32 devices in a mesh: groups: 2 (over y), particle: 4 (over z), cuts: 2 (over x), sub: 2 (over core).
Axes of the slice: x: 2, y: 2, z: 4, core: 2. Of those that a mesh axis runs over, the one named last changes fastest.
Arguments:
- weights: float32 [32, 512, 512], P(('groups', 'particle', 'cuts', 'sub')), parts along dimension 0, may hold values from -32 to 32, as said below
- features: float32 [2048, 512], P('groups'), parts along dimension 0, may hold values from -0.25 to 0.25
- targets: float32 [2048, 512], P('groups'), parts along dimension 0, may hold values from -6 to 6
Outputs:
- update: float32 [32, 512, 512], P(('groups', 'particle', 'cuts', 'sub')), parts along dimension 0
The draws below stay inside these ranges and needn't reach their ends.
There are 2 independent parts, one for each index of `groups`. The reference program is written for one: setup_inputs(seed, part) draws one part's arguments, and reference() takes and returns one part's arrays. A program takes and returns all parts, laid end to end along the dimension named above; each array names one. Nothing has to cross between parts.
Inputs may be any that keep to these rules, and one draw needn't show every extreme that they name: `weights`: parameters of every particle are of order one.
All inputs are finite; a program needn't handle non-finite values.
Results may differ from the reference program's by a relative error of at most 0.000068.
Values sent between devices are 32-bit elements; how exact they have to be, the bound alone decides.
A program may use at most 64 MiB of HBM per device.

```python
import math
import jax
import jax.numpy as jnp
from jax import lax

F = 512
NB = 512
BATCH = 1024
PARTICLES = 16


def draw_weights(key, part):
    key = jax.random.fold_in(key, 7)
    key_a, key_b, key_c, key_d = jax.random.split(key, 4)
    centre = jnp.clip(jax.random.normal(key_a, (F, NB)), -6.0, 6.0)
    spread = jnp.exp(jax.random.uniform(key_b, (PARTICLES, 1, 1), minval=math.log(0.25), maxval=math.log(2.5)))
    noise = jnp.clip(jax.random.normal(key_d, (PARTICLES, F, NB)), -4.0, 4.0)
    ramp = jnp.exp(math.log(3.0) * jnp.arange(F, dtype=jnp.float32) / F)
    jitter = jnp.exp(jax.random.uniform(key_c, (F,), minval=-0.35, maxval=0.35))
    row_scale = 0.6 * ramp * jitter
    return (centre[None, :, :] + spread * row_scale[None, :, None] * noise).astype(jnp.float32)


def normal_values(own_key, extent, scale, bound, kind=jnp.bfloat16):
    values = jax.random.normal(own_key, extent, jnp.float32) * scale
    return jnp.minimum(jnp.maximum(values, -bound), bound).astype(kind)


def setup_inputs(seed: int = 0, part: int = 0) -> dict:
    key_of = jax.random.split(jax.random.key(seed), 4)
    part_keys = jax.random.split(jax.random.fold_in(key_of[3], part), 4)
    weights = draw_weights(jax.random.fold_in(jax.random.fold_in(key_of[3], part), 71), part)
    features = normal_values(part_keys[1], (BATCH, F), F ** -0.5, 0.25, jnp.float32)
    targets = normal_values(part_keys[2], (BATCH, NB), 1.0, 6.0, jnp.float32)
    return dict(weights=weights, features=features, targets=targets)


def reference(weights, features, targets):
    highest = lax.Precision.HIGHEST
    count = PARTICLES
    width = F * NB

    def posterior_grad(params):
        misfit = targets - jnp.dot(features, params, precision=highest)
        return jnp.dot(features.T, misfit, precision=highest) - params
    grads = lax.map(posterior_grad, weights).reshape(count, width)
    flat = weights.reshape(count, width)
    gram = jnp.dot(flat, flat.T, precision=highest)
    diagonal = jnp.diagonal(gram)
    mean_sq = (diagonal[:, None] + diagonal[None, :] - 2.0 * gram) / width
    scale = jnp.sum(mean_sq) / (count * (count - 1)) + 1e-06
    kernel = jnp.exp(-math.log(count) * mean_sq / scale)
    row_total = lax.optimization_barrier(jnp.sum(kernel, axis=1))
    drive = jnp.dot(kernel, grads, precision=highest)
    pull = jnp.dot(kernel, flat, precision=highest)
    update = (drive + (row_total[:, None] * flat - pull) / scale) / row_total[:, None]
    return update.reshape(weights.shape)
```

```python
import functools
import math

import jax
import jax.numpy as jnp
from jax import lax
from jax.experimental import pallas as pl
from jax.experimental.pallas import tpu as pltpu
from jax.sharding import PartitionSpec as P

epsilon = 1e-06
HIGHEST = lax.Precision.HIGHEST
AXES = ("particle", "cuts", "sub")
PARTS = 2


def dot(a, b, contract=((1,), (0,))):
    return lax.dot_general(
        a, b, (contract, ((), ())), precision=HIGHEST, preferred_element_type=jnp.float32
    )


def kernel_weights(gram, count, width):
    row = lax.broadcasted_iota(jnp.int32, gram.shape, 0)
    col = lax.broadcasted_iota(jnp.int32, gram.shape, 1)
    diagonal = jnp.where(row == col, gram, 0.0)
    own = jnp.sum(diagonal, axis=1, keepdims=True)
    other = jnp.sum(diagonal, axis=0, keepdims=True)
    mean_sq = jnp.where(col < count, (own + other - 2.0 * gram) / width, 0.0)
    scale = jnp.sum(mean_sq, keepdims=True) / (count * (count - 1)) + epsilon
    kernel_mat = jnp.where(col < count, jnp.exp(-math.log(count) * mean_sq / scale), 0.0)
    return kernel_mat / jnp.sum(kernel_mat, axis=1, keepdims=True), scale


def body(sizes, w_hbm, x_hbm, t_hbm, out_hbm,
         w_v, x_v, t_v, slab, mixed, p_v, gram_own, gram_all, second, cross, out_v,
         local_sem, out_sem, send_w, recv_w, send_g, recv_g, send_p, recv_p):
    n_particle, n_cuts, n_sub = sizes
    count = n_particle * n_cuts * n_sub
    feats, beams = w_hbm.shape
    half = feats // PARTS
    rows = half // count
    group = lax.axis_index("groups")
    mine = [lax.axis_index(name) for name in AXES]
    me = (mine[0] * n_cuts + mine[1]) * n_sub + mine[2]

    def peer(k):
        k = count - 1 - k
        z = lax.rem(mine[0] + k // (n_cuts * n_sub), n_particle)
        x = lax.rem(mine[1] + lax.rem(k // n_sub, n_cuts), n_cuts)
        c = lax.rem(mine[2] + lax.rem(k, n_sub), n_sub)
        return (group, z, x, c), (z * n_cuts + x) * n_sub + c

    def each_peer(step):
        def go(k, carry):
            step(*peer(k))
            return carry
        lax.fori_loop(0, count - 1, go, 0)

    def place(part, index):
        return pl.ds(pl.multiple_of(part * half + index * rows, rows), rows)

    def block(index):
        return pl.ds(pl.multiple_of(index * rows, rows), rows)

    def copy_w(part, device, to, frm):
        return pltpu.make_async_remote_copy(
            src_ref=w_hbm.at[place(part, to)], dst_ref=slab.at[part, block(frm)],
            send_sem=send_w.at[part, to], recv_sem=recv_w.at[part, frm],
            device_id=device, device_id_type=pl.DeviceIdType.MESH)

    def copy_g(device, to, frm):
        return pltpu.make_async_remote_copy(
            src_ref=gram_own, dst_ref=gram_all.at[frm],
            send_sem=send_g.at[to], recv_sem=recv_g.at[frm],
            device_id=device, device_id_type=pl.DeviceIdType.MESH)

    def copy_p(part, device, to, frm):
        return pltpu.make_async_remote_copy(
            src_ref=mixed.at[part, block(to)], dst_ref=p_v.at[place(part, frm)],
            send_sem=send_p.at[part, to], recv_sem=recv_p.at[part, frm],
            device_id=device, device_id_type=pl.DeviceIdType.MESH)

    barrier = pltpu.get_barrier_semaphore()
    each_peer(lambda device, index: pl.semaphore_signal(
        barrier, inc=1, device_id=device, device_id_type=pl.DeviceIdType.MESH))
    loads = [
        pltpu.make_async_copy(x_hbm, x_v, local_sem.at[0]),
        pltpu.make_async_copy(t_hbm, t_v, local_sem.at[1]),
        pltpu.make_async_copy(w_hbm, w_v, local_sem.at[2]),
    ]
    own = [
        pltpu.make_async_copy(w_hbm.at[place(part, me)], slab.at[part, block(me)], local_sem.at[3 + part])
        for part in range(PARTS)
    ]
    for copy in loads + own:
        copy.start()
    pl.semaphore_wait(barrier, count - 1)
    for part in range(PARTS):
        each_peer(lambda device, index: copy_w(part, device, index, me).start())

    loads[0].wait()
    loads[1].wait()
    tile = 128

    def moments(step, carry):
        at = pl.ds(pl.multiple_of(step * tile, tile), tile)
        left = x_v[:, at]
        second[at, :] = dot(left, x_v[...], ((0,), (0,)))
        cross[at, :] = dot(left, t_v[...], ((0,), (0,)))
        return carry
    lax.fori_loop(0, feats // tile, moments, 0)

    total = jnp.zeros((half, half), jnp.float32)
    for part in range(PARTS):
        own[part].wait()
        each_peer(lambda device, index: copy_w(part, device, me, index).wait_recv())
        held = slab[part]
        total = total + dot(held, held, ((1,), (1,)))
    same = (
        lax.rem(lax.broadcasted_iota(jnp.int32, (half, half), 0), rows)
        == lax.rem(lax.broadcasted_iota(jnp.int32, (half, half), 1), rows)
    )
    lanes = gram_own.shape[1]
    total = jnp.where(same, total, 0.0).reshape(count, rows, half)
    pick = (
        lax.broadcasted_iota(jnp.int32, (half, lanes), 0) // rows
        == lax.broadcasted_iota(jnp.int32, (half, lanes), 1)
    ).astype(jnp.float32)
    gram_own[...] = dot(jnp.sum(total, axis=1), pick)
    each_peer(lambda device, index: copy_g(device, index, me).start())
    gram_all[pl.ds(me, 1)] = gram_own[...][None]
    each_peer(lambda device, index: copy_g(device, me, index).wait_recv())
    gram = jnp.sum(gram_all[...], axis=0)
    normal, scale = kernel_weights(gram, count, feats * beams)
    spread = dot(normal, pick, ((1,), (1,)))
    spread = jnp.broadcast_to(spread[:, None, :], (count, rows, half)).reshape(half, half)
    spread = jnp.where(same, spread, 0.0)
    for part in range(PARTS):
        mixed[part] = dot(spread, slab[part])
        p_v[place(part, me)] = mixed[part, block(me)]
        each_peer(lambda device, index: copy_p(part, device, index, me).start())

    loads[2].wait()
    inverse = 1.0 / scale
    out_v[...] = cross[...] + w_v[...] * inverse
    for part in range(PARTS):
        each_peer(lambda device, index: copy_p(part, device, me, index).wait_recv())
        at = pl.ds(part * half, half)
        arrived = p_v[at, :]
        out_v[...] -= dot(second[:, at], arrived)
        out_v[at, :] -= arrived * (1.0 + inverse)
    store = pltpu.make_async_copy(out_v, out_hbm, out_sem)
    store.start()

    for part in range(PARTS):
        each_peer(lambda device, index: copy_w(part, device, index, me).wait_send())
        each_peer(lambda device, index: copy_p(part, device, index, me).wait_send())
    each_peer(lambda device, index: copy_g(device, index, me).wait_send())
    store.wait()


def fused(sizes, weights, features, targets):
    count = math.prod(sizes)
    feats, beams = weights.shape[1:]
    batch = features.shape[0]
    half = feats // PARTS
    lanes = 128
    f32 = jnp.float32
    any_space = pl.BlockSpec(memory_space=pl.ANY)
    dma = pltpu.SemaphoreType.DMA
    result = pl.pallas_call(
        functools.partial(body, sizes),
        out_shape=jax.ShapeDtypeStruct((feats, beams), f32),
        in_specs=[any_space] * 3,
        out_specs=any_space,
        scratch_shapes=[
            pltpu.VMEM((feats, beams), f32),
            pltpu.VMEM((batch, feats), f32),
            pltpu.VMEM((batch, beams), f32),
            pltpu.VMEM((PARTS, half, beams), f32),
            pltpu.VMEM((PARTS, half, beams), f32),
            pltpu.VMEM((feats, beams), f32),
            pltpu.VMEM((count, lanes), f32),
            pltpu.VMEM((count, count, lanes), f32),
            pltpu.VMEM((feats, feats), f32),
            pltpu.VMEM((feats, beams), f32),
            pltpu.VMEM((feats, beams), f32),
            dma((3 + PARTS,)),
            dma,
            dma((PARTS, count)),
            dma((PARTS, count)),
            dma((count,)),
            dma((count,)),
            dma((PARTS, count)),
            dma((PARTS, count)),
        ],
        compiler_params=pltpu.CompilerParams(
            collective_id=0, has_side_effects=True, vmem_limit_bytes=40 * 1024 * 1024
        ),
    )(weights[0], features, targets)
    return result[None]


def exchanged(sizes, weights, features, targets):
    outer, inner = sizes[0] * sizes[1], sizes[2]
    count = outer * inner
    feats, beams = weights.shape[1:]
    piece = feats * beams // count
    sectioned = weights.reshape(1, outer, inner, piece)
    slab = lax.all_to_all(
        lax.all_to_all(sectioned, AXES[:2], split_axis=1, concat_axis=0, tiled=True),
        AXES[2], split_axis=2, concat_axis=1, tiled=True,
    ).reshape(count, piece)
    gram = lax.psum(dot(slab, slab, ((1,), (1,))), AXES)
    normal, scale = kernel_weights(gram, count, feats * beams)
    back = dot(normal, slab).reshape(outer, inner, 1, 1, piece)
    mean = lax.all_to_all(
        lax.all_to_all(back, AXES[:2], split_axis=0, concat_axis=2, tiled=True),
        AXES[2], split_axis=1, concat_axis=3, tiled=True,
    ).reshape(feats, beams)
    second = dot(features, features, ((0,), (0,)))
    cross = dot(features, targets, ((0,), (0,)))
    return (cross - dot(second, mean) - mean + (weights[0] - mean) / scale)[None]


def solution(mesh):
    sizes = tuple(mesh.shape[name] for name in AXES)
    count = math.prod(sizes)

    def on_device(weights, features, targets):
        feats = weights.shape[1]
        small = count <= 16 and feats % (PARTS * count * 8) == 0
        return (fused if small else exchanged)(sizes, weights, features, targets)

    placed = (
        P(("groups", "particle", "cuts", "sub"), None, None),
        P("groups", None),
        P("groups", None),
    )
    return jax.shard_map(
        on_device,
        mesh=mesh,
        in_specs=placed,
        out_specs=P(("groups", "particle", "cuts", "sub"), None, None),
        check_vma=False,
    )
```

```python
import functools
import math

import jax
import jax.numpy as jnp
from jax import lax
from jax.experimental import pallas as pl
from jax.experimental.pallas import tpu as pltpu
from jax.sharding import PartitionSpec as P

epsilon = 1e-06
HIGHEST = lax.Precision.HIGHEST
AXES = ("particle", "cuts", "sub")
PARTS = 2


def dot(a, b, contract=((1,), (0,))):
    return lax.dot_general(
        a, b, (contract, ((), ())), precision=HIGHEST, preferred_element_type=jnp.float32
    )


def kernel_weights(gram, count, width):
    row = lax.broadcasted_iota(jnp.int32, gram.shape, 0)
    col = lax.broadcasted_iota(jnp.int32, gram.shape, 1)
    diagonal = jnp.where(row == col, gram, 0.0)
    own = jnp.sum(diagonal, axis=1, keepdims=True)
    other = jnp.sum(diagonal, axis=0, keepdims=True)
    mean_sq = jnp.where(col < count, (own + other - 2.0 * gram) / width, 0.0)
    scale = jnp.sum(mean_sq, keepdims=True) / (count * (count - 1)) + epsilon
    kernel_mat = jnp.where(col < count, jnp.exp(-math.log(count) * mean_sq / scale), 0.0)
    return kernel_mat / jnp.sum(kernel_mat, axis=1, keepdims=True), scale


def body(sizes, w_hbm, x_hbm, t_hbm, out_hbm,
         w_v, x_v, t_v, slab, mixed, p_v, gram_own, gram_all, second, cross, out_v,
         local_sem, out_sem, send_w, recv_w, send_g, recv_g, send_p, recv_p):
    n_particle, n_cuts, n_sub = sizes
    count = n_particle * n_cuts * n_sub
    feats, beams = w_hbm.shape
    half = feats // PARTS
    rows = half // count
    group = lax.axis_index("groups")
    mine = [lax.axis_index(name) for name in AXES]
    me = (mine[0] * n_cuts + mine[1]) * n_sub + mine[2]

    def flipped(position, size, flip):
        out, bit = 0, 1
        while bit < size:
            digit = lax.rem(position // bit, 2)
            out = out + bit * (1 - digit if flip // bit % 2 else digit)
            bit *= 2
        return out

    along = [[flipped(at, size, flip) for flip in range(size)] for at, size in zip(mine, sizes)]
    peers = [
        ((group, z, x, c), (z * n_cuts + x) * n_sub + c)
        for z in along[0] for x in along[1] for c in along[2]
    ][1:]

    def each_peer(step):
        for device, index in peers:
            step(device, index)

    def place(part, index):
        return pl.ds(pl.multiple_of(part * half + index * rows, rows), rows)

    def block(index):
        return pl.ds(pl.multiple_of(index * rows, rows), rows)

    def copy_w(part, device, to, frm):
        return pltpu.make_async_remote_copy(
            src_ref=w_hbm.at[place(part, to)], dst_ref=slab.at[part, block(frm)],
            send_sem=send_w.at[part, to], recv_sem=recv_w.at[part, frm],
            device_id=device, device_id_type=pl.DeviceIdType.MESH)

    def copy_g(device, to, frm):
        return pltpu.make_async_remote_copy(
            src_ref=gram_own, dst_ref=gram_all.at[frm],
            send_sem=send_g.at[to], recv_sem=recv_g.at[frm],
            device_id=device, device_id_type=pl.DeviceIdType.MESH)

    def copy_p(part, device, to, frm):
        return pltpu.make_async_remote_copy(
            src_ref=mixed.at[part, block(to)], dst_ref=p_v.at[place(part, frm)],
            send_sem=send_p.at[part, to], recv_sem=recv_p.at[part, frm],
            device_id=device, device_id_type=pl.DeviceIdType.MESH)

    barrier = pltpu.get_barrier_semaphore()
    each_peer(lambda device, index: pl.semaphore_signal(
        barrier, inc=1, device_id=device, device_id_type=pl.DeviceIdType.MESH))
    loads = [
        pltpu.make_async_copy(x_hbm, x_v, local_sem.at[0]),
        pltpu.make_async_copy(t_hbm, t_v, local_sem.at[1]),
        pltpu.make_async_copy(w_hbm, w_v, local_sem.at[2]),
    ]
    own = [
        pltpu.make_async_copy(w_hbm.at[place(part, me)], slab.at[part, block(me)], local_sem.at[3 + part])
        for part in range(PARTS)
    ]
    for copy in loads + own:
        copy.start()
    pl.semaphore_wait(barrier, count - 1)
    for part in range(PARTS):
        each_peer(lambda device, index: copy_w(part, device, index, me).start())

    loads[0].wait()
    loads[1].wait()
    tile = 128

    def moments(step, carry):
        at = pl.ds(pl.multiple_of(step * tile, tile), tile)
        left = x_v[:, at]
        second[at, :] = dot(left, x_v[...], ((0,), (0,)))
        cross[at, :] = dot(left, t_v[...], ((0,), (0,)))
        return carry
    lax.fori_loop(0, feats // tile, moments, 0)

    total = jnp.zeros((half, half), jnp.float32)
    for part in range(PARTS):
        own[part].wait()
        each_peer(lambda device, index: copy_w(part, device, me, index).wait_recv())
        held = slab[part]
        total = total + dot(held, held, ((1,), (1,)))
    same = (
        lax.rem(lax.broadcasted_iota(jnp.int32, (half, half), 0), rows)
        == lax.rem(lax.broadcasted_iota(jnp.int32, (half, half), 1), rows)
    )
    flat = gram_own.shape[1]
    lanes = 128
    total = jnp.sum(jnp.where(same, total, 0.0).reshape(count, rows, half), axis=1)
    to_flat = (
        lax.broadcasted_iota(jnp.int32, (half, flat), 0) // rows
        == lax.rem(lax.broadcasted_iota(jnp.int32, (half, flat), 1), count)
    ).astype(jnp.float32)
    on_row = (
        lax.broadcasted_iota(jnp.int32, (count, flat), 1) // count
        == lax.broadcasted_iota(jnp.int32, (count, flat), 0)
    )
    gram_own[...] = jnp.sum(jnp.where(on_row, dot(total, to_flat), 0.0), axis=0, keepdims=True)
    each_peer(lambda device, index: copy_g(device, index, me).start())
    gram_all[pl.ds(me, 1)] = gram_own[...][None]
    each_peer(lambda device, index: copy_g(device, me, index).wait_recv())
    gram = jnp.where(on_row, jnp.broadcast_to(jnp.sum(gram_all[...], axis=0), (count, flat)), 0.0)
    from_flat = (
        lax.rem(lax.broadcasted_iota(jnp.int32, (flat, lanes), 0), count)
        == lax.broadcasted_iota(jnp.int32, (flat, lanes), 1)
    ).astype(jnp.float32)
    gram = dot(gram, from_flat)
    pick = (
        lax.broadcasted_iota(jnp.int32, (half, lanes), 0) // rows
        == lax.broadcasted_iota(jnp.int32, (half, lanes), 1)
    ).astype(jnp.float32)
    normal, scale = kernel_weights(gram, count, feats * beams)
    spread = dot(normal, pick, ((1,), (1,)))
    spread = jnp.broadcast_to(spread[:, None, :], (count, rows, half)).reshape(half, half)
    spread = jnp.where(same, spread, 0.0)
    for part in range(PARTS):
        mixed[part] = dot(spread, slab[part])
        p_v[place(part, me)] = mixed[part, block(me)]
        each_peer(lambda device, index: copy_p(part, device, index, me).start())

    loads[2].wait()
    inverse = 1.0 / scale
    out_v[...] = cross[...] + w_v[...] * inverse
    for part in range(PARTS):
        each_peer(lambda device, index: copy_p(part, device, me, index).wait_recv())
        at = pl.ds(part * half, half)
        arrived = p_v[at, :]
        out_v[...] -= dot(second[:, at], arrived)
        out_v[at, :] -= arrived * (1.0 + inverse)
    store = pltpu.make_async_copy(out_v, out_hbm, out_sem)
    store.start()

    for part in range(PARTS):
        each_peer(lambda device, index: copy_w(part, device, index, me).wait_send())
        each_peer(lambda device, index: copy_p(part, device, index, me).wait_send())
    each_peer(lambda device, index: copy_g(device, index, me).wait_send())
    store.wait()


def fused(sizes, weights, features, targets):
    count = math.prod(sizes)
    feats, beams = weights.shape[1:]
    batch = features.shape[0]
    half = feats // PARTS
    flat = max(count * count, 128)
    f32 = jnp.float32
    any_space = pl.BlockSpec(memory_space=pl.ANY)
    dma = pltpu.SemaphoreType.DMA
    result = pl.pallas_call(
        functools.partial(body, sizes),
        out_shape=jax.ShapeDtypeStruct((feats, beams), f32),
        in_specs=[any_space] * 3,
        out_specs=any_space,
        scratch_shapes=[
            pltpu.VMEM((feats, beams), f32),
            pltpu.VMEM((batch, feats), f32),
            pltpu.VMEM((batch, beams), f32),
            pltpu.VMEM((PARTS, half, beams), f32),
            pltpu.VMEM((PARTS, half, beams), f32),
            pltpu.VMEM((feats, beams), f32),
            pltpu.VMEM((1, flat), f32),
            pltpu.VMEM((count, 1, flat), f32),
            pltpu.VMEM((feats, feats), f32),
            pltpu.VMEM((feats, beams), f32),
            pltpu.VMEM((feats, beams), f32),
            dma((3 + PARTS,)),
            dma,
            dma((PARTS, count)),
            dma((PARTS, count)),
            dma((count,)),
            dma((count,)),
            dma((PARTS, count)),
            dma((PARTS, count)),
        ],
        compiler_params=pltpu.CompilerParams(
            collective_id=0, has_side_effects=True, vmem_limit_bytes=60 * 1024 * 1024
        ),
    )(weights[0], features, targets)
    return result[None]


def exchanged(sizes, weights, features, targets):
    outer, inner = sizes[0] * sizes[1], sizes[2]
    count = outer * inner
    feats, beams = weights.shape[1:]
    piece = feats * beams // count
    sectioned = weights.reshape(1, outer, inner, piece)
    slab = lax.all_to_all(
        lax.all_to_all(sectioned, AXES[:2], split_axis=1, concat_axis=0, tiled=True),
        AXES[2], split_axis=2, concat_axis=1, tiled=True,
    ).reshape(count, piece)
    gram = lax.psum(dot(slab, slab, ((1,), (1,))), AXES)
    normal, scale = kernel_weights(gram, count, feats * beams)
    back = dot(normal, slab).reshape(outer, inner, 1, 1, piece)
    mean = lax.all_to_all(
        lax.all_to_all(back, AXES[:2], split_axis=0, concat_axis=2, tiled=True),
        AXES[2], split_axis=1, concat_axis=3, tiled=True,
    ).reshape(feats, beams)
    second = dot(features, features, ((0,), (0,)))
    cross = dot(features, targets, ((0,), (0,)))
    return (cross - dot(second, mean) - mean + (weights[0] - mean) / scale)[None]


def solution(mesh):
    sizes = tuple(mesh.shape[name] for name in AXES)
    count = math.prod(sizes)

    def on_device(weights, features, targets):
        feats = weights.shape[1]
        small = count <= 16 and feats % (PARTS * count * 8) == 0
        small = small and all(size & (size - 1) == 0 for size in sizes)
        return (fused if small else exchanged)(sizes, weights, features, targets)

    placed = (
        P(("groups", "particle", "cuts", "sub"), None, None),
        P("groups", None),
        P("groups", None),
    )
    return jax.shard_map(
        on_device,
        mesh=mesh,
        in_specs=placed,
        out_specs=P(("groups", "particle", "cuts", "sub"), None, None),
        check_vma=False,
    )
```

```python
import functools
import math

import jax
import jax.numpy as jnp
from jax import lax
from jax.experimental import pallas as pl
from jax.experimental.pallas import tpu as pltpu
from jax.sharding import PartitionSpec as P

epsilon = 1e-06
HIGHEST = lax.Precision.HIGHEST
AXES = ("particle", "cuts", "sub")
PARTS = 2


def dot(a, b, contract=((1,), (0,))):
    return lax.dot_general(
        a, b, (contract, ((), ())), precision=HIGHEST, preferred_element_type=jnp.float32
    )


def pick_columns(a, chosen):
    terms, rest = [], a
    for _ in range(3):
        terms.append(rest.astype(jnp.bfloat16))
        rest = rest - terms[-1].astype(jnp.float32)
    out = jnp.dot(
        jnp.concatenate(terms, axis=0), chosen.astype(jnp.float32).astype(jnp.bfloat16),
        preferred_element_type=jnp.float32,
    ).reshape(3, a.shape[0], chosen.shape[1])
    return out[0] + (out[1] + out[2])


def kernel_weights(gram, count, width):
    row = lax.broadcasted_iota(jnp.int32, gram.shape, 0)
    col = lax.broadcasted_iota(jnp.int32, gram.shape, 1)
    diagonal = jnp.where(row == col, gram, 0.0)
    own = jnp.sum(diagonal, axis=1, keepdims=True)
    other = jnp.sum(diagonal, axis=0, keepdims=True)
    mean_sq = jnp.where(col < count, (own + other - 2.0 * gram) / width, 0.0)
    scale = jnp.sum(mean_sq, keepdims=True) / (count * (count - 1)) + epsilon
    kernel_mat = jnp.where(col < count, jnp.exp(-math.log(count) * mean_sq / scale), 0.0)
    return kernel_mat / jnp.sum(kernel_mat, axis=1, keepdims=True), scale


def body(sizes, w_hbm, x_hbm, t_hbm, out_v,
         w_v, x_v, t_v, slab, mixed, p_v, gram_own, gram_all, second, cross,
         local_sem, send_w, recv_w, send_g, recv_g, send_p, recv_p):
    n_particle, n_cuts, n_sub = sizes
    count = n_particle * n_cuts * n_sub
    feats, beams = w_hbm.shape
    half = feats // PARTS
    rows = half // count
    group = lax.axis_index("groups")
    mine = [lax.axis_index(name) for name in AXES]
    me = (mine[0] * n_cuts + mine[1]) * n_sub + mine[2]

    def flipped(position, size, flip):
        out, bit = 0, 1
        while bit < size:
            digit = lax.rem(position // bit, 2)
            out = out + bit * (1 - digit if flip // bit % 2 else digit)
            bit *= 2
        return out

    along = [[flipped(at, size, flip) for flip in range(size)] for at, size in zip(mine, sizes)]
    peers = [
        ((group, z, x, c), (z * n_cuts + x) * n_sub + c)
        for z in along[0] for x in along[1] for c in along[2]
    ][1:]

    def each_peer(step):
        for device, index in peers:
            step(device, index)

    def place(part, index):
        return pl.ds(pl.multiple_of(part * half + index * rows, rows), rows)

    def block(index):
        return pl.ds(pl.multiple_of(index * rows, rows), rows)

    def copy_w(part, device, to, frm):
        return pltpu.make_async_remote_copy(
            src_ref=w_hbm.at[place(part, to)], dst_ref=slab.at[part, block(frm)],
            send_sem=send_w.at[part, to], recv_sem=recv_w.at[part, frm],
            device_id=device, device_id_type=pl.DeviceIdType.MESH)

    def copy_g(device, to, frm):
        return pltpu.make_async_remote_copy(
            src_ref=gram_own, dst_ref=gram_all.at[frm],
            send_sem=send_g.at[to], recv_sem=recv_g.at[frm],
            device_id=device, device_id_type=pl.DeviceIdType.MESH)

    def copy_p(part, device, to, frm):
        return pltpu.make_async_remote_copy(
            src_ref=mixed.at[part, block(to)], dst_ref=p_v.at[place(part, frm)],
            send_sem=send_p.at[part, to], recv_sem=recv_p.at[part, frm],
            device_id=device, device_id_type=pl.DeviceIdType.MESH)

    barrier = pltpu.get_barrier_semaphore()
    each_peer(lambda device, index: pl.semaphore_signal(
        barrier, inc=1, device_id=device, device_id_type=pl.DeviceIdType.MESH))
    loads = [
        pltpu.make_async_copy(x_hbm, x_v, local_sem.at[0]),
        pltpu.make_async_copy(t_hbm, t_v, local_sem.at[1]),
        pltpu.make_async_copy(w_hbm, w_v, local_sem.at[2]),
    ]
    own = [
        pltpu.make_async_copy(w_hbm.at[place(part, me)], slab.at[part, block(me)], local_sem.at[3 + part])
        for part in range(PARTS)
    ]
    for copy in loads + own:
        copy.start()
    pl.semaphore_wait(barrier, count - 1)
    for part in range(PARTS):
        each_peer(lambda device, index: copy_w(part, device, index, me).start())

    loads[0].wait()
    loads[1].wait()
    tile = 128

    def moments(step, carry):
        at = pl.ds(pl.multiple_of(step * tile, tile), tile)
        left = x_v[:, at]
        second[at, :] = dot(left, x_v[...], ((0,), (0,)))
        cross[at, :] = dot(left, t_v[...], ((0,), (0,)))
        return carry
    lax.fori_loop(0, feats // tile, moments, 0)

    total = jnp.zeros((half, half), jnp.float32)
    for part in range(PARTS):
        own[part].wait()
        each_peer(lambda device, index: copy_w(part, device, me, index).wait_recv())
        held = slab[part]
        total = total + dot(held, held, ((1,), (1,)))
    same = (
        lax.rem(lax.broadcasted_iota(jnp.int32, (half, half), 0), rows)
        == lax.rem(lax.broadcasted_iota(jnp.int32, (half, half), 1), rows)
    )
    flat = gram_own.shape[1]
    lanes = 128
    total = jnp.sum(jnp.where(same, total, 0.0).reshape(count, rows, half), axis=1)
    to_flat = (
        lax.broadcasted_iota(jnp.int32, (half, flat), 0) // rows
        == lax.rem(lax.broadcasted_iota(jnp.int32, (half, flat), 1), count)
    )
    on_row = (
        lax.broadcasted_iota(jnp.int32, (count, flat), 1) // count
        == lax.broadcasted_iota(jnp.int32, (count, flat), 0)
    )
    gram_own[...] = jnp.sum(jnp.where(on_row, pick_columns(total, to_flat), 0.0), axis=0, keepdims=True)
    each_peer(lambda device, index: copy_g(device, index, me).start())
    gram_all[pl.ds(me, 1)] = gram_own[...][None]
    each_peer(lambda device, index: copy_g(device, me, index).wait_recv())
    gram = jnp.where(on_row, jnp.broadcast_to(jnp.sum(gram_all[...], axis=0), (count, flat)), 0.0)
    from_flat = (
        lax.rem(lax.broadcasted_iota(jnp.int32, (flat, lanes), 0), count)
        == lax.broadcasted_iota(jnp.int32, (flat, lanes), 1)
    )
    gram = pick_columns(gram, from_flat)
    to_rows = (
        lax.broadcasted_iota(jnp.int32, (lanes, half), 1) // rows
        == lax.broadcasted_iota(jnp.int32, (lanes, half), 0)
    )
    normal, scale = kernel_weights(gram, count, feats * beams)
    spread = pick_columns(normal, to_rows)
    spread = jnp.broadcast_to(spread[:, None, :], (count, rows, half)).reshape(half, half)
    spread = jnp.where(same, spread, 0.0)
    for part in range(PARTS):
        mixed[part] = dot(spread, slab[part])
        p_v[place(part, me)] = mixed[part, block(me)]
        each_peer(lambda device, index: copy_p(part, device, index, me).start())

    loads[2].wait()
    inverse = 1.0 / scale
    out_v[...] = cross[...] + w_v[...] * inverse
    for part in range(PARTS):
        each_peer(lambda device, index: copy_p(part, device, me, index).wait_recv())
        at = pl.ds(part * half, half)
        arrived = p_v[at, :]
        out_v[...] -= dot(second[:, at], arrived)
        out_v[at, :] -= arrived * (1.0 + inverse)

    for part in range(PARTS):
        each_peer(lambda device, index: copy_w(part, device, index, me).wait_send())
        each_peer(lambda device, index: copy_p(part, device, index, me).wait_send())
    each_peer(lambda device, index: copy_g(device, index, me).wait_send())


def fused(sizes, weights, features, targets):
    count = math.prod(sizes)
    feats, beams = weights.shape[1:]
    batch = features.shape[0]
    half = feats // PARTS
    flat = max(count * count, 128)
    f32 = jnp.float32
    dma = pltpu.SemaphoreType.DMA
    result = pl.pallas_call(
        functools.partial(body, sizes),
        out_shape=jax.ShapeDtypeStruct((feats, beams), f32),
        in_specs=[pl.BlockSpec(memory_space=pltpu.HBM)] * 3,
        out_specs=pl.BlockSpec(memory_space=pltpu.VMEM),
        scratch_shapes=[
            pltpu.VMEM((feats, beams), f32),
            pltpu.VMEM((batch, feats), f32),
            pltpu.VMEM((batch, beams), f32),
            pltpu.VMEM((PARTS, half, beams), f32),
            pltpu.VMEM((PARTS, half, beams), f32),
            pltpu.VMEM((feats, beams), f32),
            pltpu.VMEM((1, flat), f32),
            pltpu.VMEM((count, 1, flat), f32),
            pltpu.VMEM((feats, feats), f32),
            pltpu.VMEM((feats, beams), f32),
            dma((3 + PARTS,)),
            dma((PARTS, count)),
            dma((PARTS, count)),
            dma((count,)),
            dma((count,)),
            dma((PARTS, count)),
            dma((PARTS, count)),
        ],
        compiler_params=pltpu.CompilerParams(
            collective_id=0, has_side_effects=True, vmem_limit_bytes=52 * 1024 * 1024
        ),
    )(weights[0], features, targets)
    return result[None]


def exchanged(sizes, weights, features, targets):
    outer, inner = sizes[0] * sizes[1], sizes[2]
    count = outer * inner
    feats, beams = weights.shape[1:]
    piece = feats * beams // count
    sectioned = weights.reshape(1, outer, inner, piece)
    slab = lax.all_to_all(
        lax.all_to_all(sectioned, AXES[:2], split_axis=1, concat_axis=0, tiled=True),
        AXES[2], split_axis=2, concat_axis=1, tiled=True,
    ).reshape(count, piece)
    gram = lax.psum(dot(slab, slab, ((1,), (1,))), AXES)
    normal, scale = kernel_weights(gram, count, feats * beams)
    back = dot(normal, slab).reshape(outer, inner, 1, 1, piece)
    mean = lax.all_to_all(
        lax.all_to_all(back, AXES[:2], split_axis=0, concat_axis=2, tiled=True),
        AXES[2], split_axis=1, concat_axis=3, tiled=True,
    ).reshape(feats, beams)
    second = dot(features, features, ((0,), (0,)))
    cross = dot(features, targets, ((0,), (0,)))
    return (cross - dot(second, mean) - mean + (weights[0] - mean) / scale)[None]


def solution(mesh):
    sizes = tuple(mesh.shape[name] for name in AXES)
    count = math.prod(sizes)

    def on_device(weights, features, targets):
        feats = weights.shape[1]
        small = count <= 16 and feats % (PARTS * count * 8) == 0
        small = small and all(size & (size - 1) == 0 for size in sizes)
        return (fused if small else exchanged)(sizes, weights, features, targets)

    placed = (
        P(("groups", "particle", "cuts", "sub"), None, None),
        P("groups", None),
        P("groups", None),
    )
    return jax.shard_map(
        on_device,
        mesh=mesh,
        in_specs=placed,
        out_specs=P(("groups", "particle", "cuts", "sub"), None, None),
        check_vma=False,
    )
```

```python
import functools
import math

import jax
import jax.numpy as jnp
from jax import lax
from jax.experimental import pallas as pl
from jax.experimental.pallas import tpu as pltpu
from jax.sharding import PartitionSpec as P

epsilon = 1e-06
HIGHEST = lax.Precision.HIGHEST
AXES = ("particle", "cuts", "sub")
PARTS = 2


def dot(a, b, contract=((1,), (0,))):
    return lax.dot_general(
        a, b, (contract, ((), ())), precision=HIGHEST, preferred_element_type=jnp.float32
    )


def pick_columns(a, chosen):
    terms, rest = [], a
    for _ in range(3):
        terms.append(rest.astype(jnp.bfloat16))
        rest = rest - terms[-1].astype(jnp.float32)
    out = jnp.dot(
        jnp.concatenate(terms, axis=0), chosen.astype(jnp.float32).astype(jnp.bfloat16),
        preferred_element_type=jnp.float32,
    ).reshape(3, a.shape[0], chosen.shape[1])
    return out[0] + (out[1] + out[2])


def kernel_weights(gram, count, width):
    row = lax.broadcasted_iota(jnp.int32, gram.shape, 0)
    col = lax.broadcasted_iota(jnp.int32, gram.shape, 1)
    diagonal = jnp.where(row == col, gram, 0.0)
    own = jnp.sum(diagonal, axis=1, keepdims=True)
    other = jnp.sum(diagonal, axis=0, keepdims=True)
    mean_sq = jnp.where(col < count, (own + other - 2.0 * gram) / width, 0.0)
    scale = jnp.sum(mean_sq, keepdims=True) / (count * (count - 1)) + epsilon
    kernel_mat = jnp.where(col < count, jnp.exp(-math.log(count) * mean_sq / scale), 0.0)
    return kernel_mat / jnp.sum(kernel_mat, axis=1, keepdims=True), scale


def body(sizes, w_hbm, x_hbm, t_hbm, out_v,
         w_v, x_v, t_v, slab, mixed, p_v, gram_own, gram_all, second, cross,
         local_sem, send_w, recv_w, send_g, recv_g, send_p, recv_p):
    n_particle, n_cuts, n_sub = sizes
    count = n_particle * n_cuts * n_sub
    feats, beams = w_hbm.shape
    half = feats // PARTS
    rows = half // count
    group = lax.axis_index("groups")
    mine = [lax.axis_index(name) for name in AXES]
    me = (mine[0] * n_cuts + mine[1]) * n_sub + mine[2]

    def flipped(position, size, flip):
        out, bit = 0, 1
        while bit < size:
            digit = lax.rem(position // bit, 2)
            out = out + bit * (1 - digit if flip // bit % 2 else digit)
            bit *= 2
        return out

    along = [[flipped(at, size, flip) for flip in range(size)] for at, size in zip(mine, sizes)]
    peers = [
        ((group, z, x, c), (z * n_cuts + x) * n_sub + c)
        for z in along[0] for x in along[1] for c in along[2]
    ][1:]

    def each_peer(step):
        for device, index in peers:
            step(device, index)

    def place(part, index):
        return pl.ds(pl.multiple_of(part * half + index * rows, rows), rows)

    def block(index):
        return pl.ds(pl.multiple_of(index * rows, rows), rows)

    def copy_w(part, device, to, frm):
        return pltpu.make_async_remote_copy(
            src_ref=w_hbm.at[place(part, to)], dst_ref=slab.at[part, block(frm)],
            send_sem=send_w.at[part, to], recv_sem=recv_w.at[part, frm],
            device_id=device, device_id_type=pl.DeviceIdType.MESH)

    def copy_g(device, to, frm):
        return pltpu.make_async_remote_copy(
            src_ref=gram_own, dst_ref=gram_all.at[frm],
            send_sem=send_g.at[to], recv_sem=recv_g.at[frm],
            device_id=device, device_id_type=pl.DeviceIdType.MESH)

    def copy_p(part, device, to, frm):
        return pltpu.make_async_remote_copy(
            src_ref=mixed.at[part, block(to)], dst_ref=p_v.at[place(part, frm)],
            send_sem=send_p.at[part, to], recv_sem=recv_p.at[part, frm],
            device_id=device, device_id_type=pl.DeviceIdType.MESH)

    barrier = pltpu.get_barrier_semaphore()
    each_peer(lambda device, index: pl.semaphore_signal(
        barrier, inc=1, device_id=device, device_id_type=pl.DeviceIdType.MESH))
    loads = [
        pltpu.make_async_copy(x_hbm, x_v, local_sem.at[0]),
        pltpu.make_async_copy(t_hbm, t_v, local_sem.at[1]),
        pltpu.make_async_copy(w_hbm, w_v, local_sem.at[2]),
    ]
    own = [
        pltpu.make_async_copy(w_hbm.at[place(part, me)], slab.at[part, block(me)], local_sem.at[3 + part])
        for part in range(PARTS)
    ]
    for copy in loads + own:
        copy.start()
    pl.semaphore_wait(barrier, count - 1)
    for part in range(PARTS):
        each_peer(lambda device, index: copy_w(part, device, index, me).start())

    loads[0].wait()
    loads[1].wait()
    tile = 128

    def moments(step, carry):
        at = pl.ds(pl.multiple_of(step * tile, tile), tile)
        left = x_v[:, at]
        second[at, :] = dot(left, x_v[...], ((0,), (0,)))
        cross[at, :] = dot(left, t_v[...], ((0,), (0,)))
        return carry
    lax.fori_loop(0, feats // tile, moments, 0)

    total = jnp.zeros((half, half), jnp.float32)
    for part in range(PARTS):
        own[part].wait()
        each_peer(lambda device, index: copy_w(part, device, me, index).wait_recv())
        held = slab[part]
        total = total + dot(held, held, ((1,), (1,)))
    same = (
        lax.rem(lax.broadcasted_iota(jnp.int32, (half, half), 0), rows)
        == lax.rem(lax.broadcasted_iota(jnp.int32, (half, half), 1), rows)
    )
    flat = gram_own.shape[1]
    lanes = 128
    total = jnp.sum(jnp.where(same, total, 0.0).reshape(count, rows, half), axis=1)
    to_flat = (
        lax.broadcasted_iota(jnp.int32, (half, flat), 0) // rows
        == lax.rem(lax.broadcasted_iota(jnp.int32, (half, flat), 1), count)
    )
    on_row = (
        lax.broadcasted_iota(jnp.int32, (count, flat), 1) // count
        == lax.broadcasted_iota(jnp.int32, (count, flat), 0)
    )
    gram_own[...] = jnp.sum(jnp.where(on_row, pick_columns(total, to_flat), 0.0), axis=0, keepdims=True)
    each_peer(lambda device, index: copy_g(device, index, me).start())
    gram_all[pl.ds(me, 1)] = gram_own[...][None]
    each_peer(lambda device, index: copy_g(device, me, index).wait_recv())
    gram = jnp.where(on_row, jnp.broadcast_to(jnp.sum(gram_all[...], axis=0), (count, flat)), 0.0)
    from_flat = (
        lax.rem(lax.broadcasted_iota(jnp.int32, (flat, lanes), 0), count)
        == lax.broadcasted_iota(jnp.int32, (flat, lanes), 1)
    )
    gram = pick_columns(gram, from_flat)
    to_rows = (
        lax.broadcasted_iota(jnp.int32, (lanes, half), 1) // rows
        == lax.broadcasted_iota(jnp.int32, (lanes, half), 0)
    )
    normal, scale = kernel_weights(gram, count, feats * beams)
    spread = pick_columns(normal, to_rows)
    spread = jnp.broadcast_to(spread[:, None, :], (count, rows, half)).reshape(half, half)
    spread = jnp.where(same, spread, 0.0)
    for part in range(PARTS):
        mixed[part] = dot(spread, slab[part])
        each_peer(lambda device, index: copy_p(part, device, index, me).start())
        p_v[place(part, me)] = mixed[part, block(me)]

    for part in range(PARTS):
        each_peer(lambda device, index: copy_w(part, device, index, me).wait_send())
    each_peer(lambda device, index: copy_g(device, index, me).wait_send())
    loads[2].wait()
    inverse = 1.0 / scale
    out_v[...] = cross[...] + w_v[...] * inverse
    for part in range(PARTS):
        each_peer(lambda device, index: copy_p(part, device, me, index).wait_recv())
        at = pl.ds(part * half, half)
        arrived = p_v[at, :]
        out_v[...] -= dot(second[:, at], arrived)
        out_v[at, :] -= arrived * (1.0 + inverse)
        each_peer(lambda device, index: copy_p(part, device, index, me).wait_send())


def fused(sizes, weights, features, targets):
    count = math.prod(sizes)
    feats, beams = weights.shape[1:]
    batch = features.shape[0]
    half = feats // PARTS
    flat = max(count * count, 128)
    f32 = jnp.float32
    dma = pltpu.SemaphoreType.DMA
    result = pl.pallas_call(
        functools.partial(body, sizes),
        out_shape=jax.ShapeDtypeStruct((feats, beams), f32),
        in_specs=[pl.BlockSpec(memory_space=pltpu.HBM)] * 3,
        out_specs=pl.BlockSpec(memory_space=pltpu.VMEM),
        scratch_shapes=[
            pltpu.VMEM((feats, beams), f32),
            pltpu.VMEM((batch, feats), f32),
            pltpu.VMEM((batch, beams), f32),
            pltpu.VMEM((PARTS, half, beams), f32),
            pltpu.VMEM((PARTS, half, beams), f32),
            pltpu.VMEM((feats, beams), f32),
            pltpu.VMEM((1, flat), f32),
            pltpu.VMEM((count, 1, flat), f32),
            pltpu.VMEM((feats, feats), f32),
            pltpu.VMEM((feats, beams), f32),
            dma((3 + PARTS,)),
            dma((PARTS, count)),
            dma((PARTS, count)),
            dma((count,)),
            dma((count,)),
            dma((PARTS, count)),
            dma((PARTS, count)),
        ],
        compiler_params=pltpu.CompilerParams(
            collective_id=0, has_side_effects=True, vmem_limit_bytes=52 * 1024 * 1024
        ),
    )(weights[0], features, targets)
    return result[None]


def exchanged(sizes, weights, features, targets):
    outer, inner = sizes[0] * sizes[1], sizes[2]
    count = outer * inner
    feats, beams = weights.shape[1:]
    piece = feats * beams // count
    sectioned = weights.reshape(1, outer, inner, piece)
    slab = lax.all_to_all(
        lax.all_to_all(sectioned, AXES[:2], split_axis=1, concat_axis=0, tiled=True),
        AXES[2], split_axis=2, concat_axis=1, tiled=True,
    ).reshape(count, piece)
    gram = lax.psum(dot(slab, slab, ((1,), (1,))), AXES)
    normal, scale = kernel_weights(gram, count, feats * beams)
    back = dot(normal, slab).reshape(outer, inner, 1, 1, piece)
    mean = lax.all_to_all(
        lax.all_to_all(back, AXES[:2], split_axis=0, concat_axis=2, tiled=True),
        AXES[2], split_axis=1, concat_axis=3, tiled=True,
    ).reshape(feats, beams)
    second = dot(features, features, ((0,), (0,)))
    cross = dot(features, targets, ((0,), (0,)))
    return (cross - dot(second, mean) - mean + (weights[0] - mean) / scale)[None]


def solution(mesh):
    sizes = tuple(mesh.shape[name] for name in AXES)
    count = math.prod(sizes)

    def on_device(weights, features, targets):
        feats = weights.shape[1]
        small = count <= 16 and feats % (PARTS * count * 8) == 0
        small = small and all(size & (size - 1) == 0 for size in sizes)
        return (fused if small else exchanged)(sizes, weights, features, targets)

    placed = (
        P(("groups", "particle", "cuts", "sub"), None, None),
        P("groups", None),
        P("groups", None),
    )
    return jax.shard_map(
        on_device,
        mesh=mesh,
        in_specs=placed,
        out_specs=P(("groups", "particle", "cuts", "sub"), None, None),
        check_vma=False,
    )
```

```python
import functools
import math

import jax
import jax.numpy as jnp
from jax import lax
from jax.experimental import pallas as pl
from jax.experimental.pallas import tpu as pltpu
from jax.sharding import PartitionSpec as P

epsilon = 1e-06
HIGHEST = lax.Precision.HIGHEST
AXES = ("particle", "cuts", "sub")
PARTS = 2


def dot(a, b, contract=((1,), (0,))):
    return lax.dot_general(
        a, b, (contract, ((), ())), precision=HIGHEST, preferred_element_type=jnp.float32
    )


def split(a):
    terms = []
    for _ in range(3):
        terms.append(a.astype(jnp.bfloat16))
        a = a - terms[-1].astype(jnp.float32)
    return terms


def pick_columns(a, chosen):
    terms, rest = [], a
    for _ in range(3):
        terms.append(rest.astype(jnp.bfloat16))
        rest = rest - terms[-1].astype(jnp.float32)
    out = jnp.dot(
        jnp.concatenate(terms, axis=0), chosen.astype(jnp.float32).astype(jnp.bfloat16),
        preferred_element_type=jnp.float32,
    ).reshape(3, a.shape[0], chosen.shape[1])
    return out[0] + (out[1] + out[2])


def kernel_weights(gram, count, width):
    row = lax.broadcasted_iota(jnp.int32, gram.shape, 0)
    col = lax.broadcasted_iota(jnp.int32, gram.shape, 1)
    diagonal = jnp.where(row == col, gram, 0.0)
    own = jnp.sum(diagonal, axis=1, keepdims=True)
    other = jnp.sum(diagonal, axis=0, keepdims=True)
    mean_sq = jnp.where(col < count, (own + other - 2.0 * gram) / width, 0.0)
    scale = jnp.sum(mean_sq, keepdims=True) / (count * (count - 1)) + epsilon
    kernel_mat = jnp.where(col < count, jnp.exp(-math.log(count) * mean_sq / scale), 0.0)
    return kernel_mat / jnp.sum(kernel_mat, axis=1, keepdims=True), scale


def body(sizes, w_hbm, x_hbm, t_hbm, out_v,
         w_v, x_v, t_v, slab, mixed, p_v, gram_own, gram_all, second, cross, left_terms,
         local_sem, send_w, recv_w, send_g, recv_g, send_p, recv_p):
    n_particle, n_cuts, n_sub = sizes
    count = n_particle * n_cuts * n_sub
    feats, beams = w_hbm.shape
    half = feats // PARTS
    rows = half // count
    group = lax.axis_index("groups")
    mine = [lax.axis_index(name) for name in AXES]
    me = (mine[0] * n_cuts + mine[1]) * n_sub + mine[2]

    def flipped(position, size, flip):
        out, bit = 0, 1
        while bit < size:
            digit = lax.rem(position // bit, 2)
            out = out + bit * (1 - digit if flip // bit % 2 else digit)
            bit *= 2
        return out

    along = [[flipped(at, size, flip) for flip in range(size)] for at, size in zip(mine, sizes)]
    peers = [
        ((group, z, x, c), (z * n_cuts + x) * n_sub + c)
        for z in along[0] for x in along[1] for c in along[2]
    ][1:]

    def each_peer(step):
        for device, index in peers:
            step(device, index)

    def place(part, index):
        return pl.ds(pl.multiple_of(part * half + index * rows, rows), rows)

    def block(index):
        return pl.ds(pl.multiple_of(index * rows, rows), rows)

    def copy_w(part, device, to, frm):
        return pltpu.make_async_remote_copy(
            src_ref=w_hbm.at[place(part, to)], dst_ref=slab.at[part, block(frm)],
            send_sem=send_w.at[part, to], recv_sem=recv_w.at[part, frm],
            device_id=device, device_id_type=pl.DeviceIdType.MESH)

    def copy_g(device, to, frm):
        return pltpu.make_async_remote_copy(
            src_ref=gram_own, dst_ref=gram_all.at[frm],
            send_sem=send_g.at[to], recv_sem=recv_g.at[frm],
            device_id=device, device_id_type=pl.DeviceIdType.MESH)

    def copy_p(part, device, to, frm):
        return pltpu.make_async_remote_copy(
            src_ref=mixed.at[part, block(to)], dst_ref=p_v.at[place(part, frm)],
            send_sem=send_p.at[part, to], recv_sem=recv_p.at[part, frm],
            device_id=device, device_id_type=pl.DeviceIdType.MESH)

    barrier = pltpu.get_barrier_semaphore()
    each_peer(lambda device, index: pl.semaphore_signal(
        barrier, inc=1, device_id=device, device_id_type=pl.DeviceIdType.MESH))
    loads = [
        pltpu.make_async_copy(x_hbm, x_v, local_sem.at[0]),
        pltpu.make_async_copy(t_hbm, t_v, local_sem.at[1]),
        pltpu.make_async_copy(w_hbm, w_v, local_sem.at[2]),
    ]
    own = [
        pltpu.make_async_copy(w_hbm.at[place(part, me)], slab.at[part, block(me)], local_sem.at[3 + part])
        for part in range(PARTS)
    ]
    for copy in loads + own:
        copy.start()
    pl.semaphore_wait(barrier, count - 1)
    for part in range(PARTS):
        each_peer(lambda device, index: copy_w(part, device, index, me).start())

    loads[0].wait()
    loads[1].wait()
    tile = 128

    def moments(step, carry):
        at = pl.ds(pl.multiple_of(step * tile, tile), tile)
        left = x_v[:, at]
        second[at, :] = dot(left, x_v[...], ((0,), (0,)))
        cross[at, :] = dot(left, t_v[...], ((0,), (0,)))
        return carry
    lax.fori_loop(0, feats // tile, moments, 0)

    for part in range(PARTS):
        a, b, c = split(second[:, pl.ds(part * half, half)])
        left_terms[part] = jnp.concatenate([a, a, a, b, b, c], axis=1)

    total = jnp.zeros((half, half), jnp.float32)
    for part in range(PARTS):
        own[part].wait()
        each_peer(lambda device, index: copy_w(part, device, me, index).wait_recv())
        held = slab[part]
        total = total + dot(held, held, ((1,), (1,)))
    same = (
        lax.rem(lax.broadcasted_iota(jnp.int32, (half, half), 0), rows)
        == lax.rem(lax.broadcasted_iota(jnp.int32, (half, half), 1), rows)
    )
    flat = gram_own.shape[1]
    lanes = 128
    total = jnp.sum(jnp.where(same, total, 0.0).reshape(count, rows, half), axis=1)
    to_flat = (
        lax.broadcasted_iota(jnp.int32, (half, flat), 0) // rows
        == lax.rem(lax.broadcasted_iota(jnp.int32, (half, flat), 1), count)
    )
    on_row = (
        lax.broadcasted_iota(jnp.int32, (count, flat), 1) // count
        == lax.broadcasted_iota(jnp.int32, (count, flat), 0)
    )
    gram_own[...] = jnp.sum(jnp.where(on_row, pick_columns(total, to_flat), 0.0), axis=0, keepdims=True)
    each_peer(lambda device, index: copy_g(device, index, me).start())
    gram_all[pl.ds(me, 1)] = gram_own[...][None]
    each_peer(lambda device, index: copy_g(device, me, index).wait_recv())
    gram = jnp.where(on_row, jnp.broadcast_to(jnp.sum(gram_all[...], axis=0), (count, flat)), 0.0)
    from_flat = (
        lax.rem(lax.broadcasted_iota(jnp.int32, (flat, lanes), 0), count)
        == lax.broadcasted_iota(jnp.int32, (flat, lanes), 1)
    )
    gram = pick_columns(gram, from_flat)
    to_rows = (
        lax.broadcasted_iota(jnp.int32, (lanes, half), 1) // rows
        == lax.broadcasted_iota(jnp.int32, (lanes, half), 0)
    )
    normal, scale = kernel_weights(gram, count, feats * beams)
    spread = pick_columns(normal, to_rows)
    spread = jnp.broadcast_to(spread[:, None, :], (count, rows, half)).reshape(half, half)
    spread = jnp.where(same, spread, 0.0)
    for part in range(PARTS):
        mixed[part] = dot(spread, slab[part])
        each_peer(lambda device, index: copy_p(part, device, index, me).start())
        p_v[place(part, me)] = mixed[part, block(me)]

    for part in range(PARTS):
        each_peer(lambda device, index: copy_w(part, device, index, me).wait_send())
    each_peer(lambda device, index: copy_g(device, index, me).wait_send())
    loads[2].wait()
    inverse = 1.0 / scale
    out_v[...] = cross[...] + w_v[...] * inverse
    for part in range(PARTS):
        each_peer(lambda device, index: copy_p(part, device, me, index).wait_recv())
        at = pl.ds(part * half, half)
        arrived = p_v[at, :]
        a, b, c = split(arrived)
        right_terms = jnp.concatenate([a, b, c, a, b, a], axis=0)
        out_v[...] -= jnp.dot(left_terms[part], right_terms, preferred_element_type=jnp.float32)
        out_v[at, :] -= arrived * (1.0 + inverse)
        each_peer(lambda device, index: copy_p(part, device, index, me).wait_send())


def fused(sizes, weights, features, targets):
    count = math.prod(sizes)
    feats, beams = weights.shape[1:]
    batch = features.shape[0]
    half = feats // PARTS
    flat = max(count * count, 128)
    f32 = jnp.float32
    dma = pltpu.SemaphoreType.DMA
    result = pl.pallas_call(
        functools.partial(body, sizes),
        out_shape=jax.ShapeDtypeStruct((feats, beams), f32),
        in_specs=[pl.BlockSpec(memory_space=pltpu.HBM)] * 3,
        out_specs=pl.BlockSpec(memory_space=pltpu.VMEM),
        scratch_shapes=[
            pltpu.VMEM((feats, beams), f32),
            pltpu.VMEM((batch, feats), f32),
            pltpu.VMEM((batch, beams), f32),
            pltpu.VMEM((PARTS, half, beams), f32),
            pltpu.VMEM((PARTS, half, beams), f32),
            pltpu.VMEM((feats, beams), f32),
            pltpu.VMEM((1, flat), f32),
            pltpu.VMEM((count, 1, flat), f32),
            pltpu.VMEM((feats, feats), f32),
            pltpu.VMEM((feats, beams), f32),
            pltpu.VMEM((PARTS, feats, 6 * half), jnp.bfloat16),
            dma((3 + PARTS,)),
            dma((PARTS, count)),
            dma((PARTS, count)),
            dma((count,)),
            dma((count,)),
            dma((PARTS, count)),
            dma((PARTS, count)),
        ],
        compiler_params=pltpu.CompilerParams(
            collective_id=0, has_side_effects=True, vmem_limit_bytes=52 * 1024 * 1024
        ),
    )(weights[0], features, targets)
    return result[None]


def exchanged(sizes, weights, features, targets):
    outer, inner = sizes[0] * sizes[1], sizes[2]
    count = outer * inner
    feats, beams = weights.shape[1:]
    piece = feats * beams // count
    sectioned = weights.reshape(1, outer, inner, piece)
    slab = lax.all_to_all(
        lax.all_to_all(sectioned, AXES[:2], split_axis=1, concat_axis=0, tiled=True),
        AXES[2], split_axis=2, concat_axis=1, tiled=True,
    ).reshape(count, piece)
    gram = lax.psum(dot(slab, slab, ((1,), (1,))), AXES)
    normal, scale = kernel_weights(gram, count, feats * beams)
    back = dot(normal, slab).reshape(outer, inner, 1, 1, piece)
    mean = lax.all_to_all(
        lax.all_to_all(back, AXES[:2], split_axis=0, concat_axis=2, tiled=True),
        AXES[2], split_axis=1, concat_axis=3, tiled=True,
    ).reshape(feats, beams)
    second = dot(features, features, ((0,), (0,)))
    cross = dot(features, targets, ((0,), (0,)))
    return (cross - dot(second, mean) - mean + (weights[0] - mean) / scale)[None]


def solution(mesh):
    sizes = tuple(mesh.shape[name] for name in AXES)
    count = math.prod(sizes)

    def on_device(weights, features, targets):
        feats = weights.shape[1]
        small = count <= 16 and feats % (PARTS * count * 8) == 0
        small = small and all(size & (size - 1) == 0 for size in sizes)
        return (fused if small else exchanged)(sizes, weights, features, targets)

    placed = (
        P(("groups", "particle", "cuts", "sub"), None, None),
        P("groups", None),
        P("groups", None),
    )
    return jax.shard_map(
        on_device,
        mesh=mesh,
        in_specs=placed,
        out_specs=P(("groups", "particle", "cuts", "sub"), None, None),
        check_vma=False,
    )
```
